512 devices in a mesh: gx: 64 (over z, x), gy: 8 (over y, core).
Axes of the slice: x: 4, y: 4, z: 16, core: 2. Of those that a mesh axis runs over, the one named last changes fastest.
Arguments:
- object_field: float32 [2, 2, 1024, 16384], P(None, None, 'gy', 'gx'), may hold values from -5 to 5
- first_moment: float32 [2, 2, 1024, 16384], P(None, None, 'gy', 'gx'), may hold values from -2 to 2
- second_moment: float32 [2, 2, 1024, 16384], P(None, None, 'gy', 'gx'), may hold values from 0.2 to 4
- probe_wave: float32 [2, 128, 128], replicated, may hold values from -5 to 5
- patterns: float32 [8, 768, 128, 128], P('gy', 'gx'), may hold values from 0.05 to 5
- row_offsets: int32 [8, 768], P('gy', 'gx'), may hold values from 0 to 127
- col_offsets: int32 [8, 768], P('gy', 'gx'), may hold values from 0 to 255
- counts: int32 [8, 64], P('gy', 'gx'), may hold values from 1 to 12, as said below
Outputs:
- new_object: float32 [2, 2, 1024, 16384], P(None, None, 'gy', 'gx')
- new_first: float32 [2, 2, 1024, 16384], P(None, None, 'gy', 'gx')
- new_second: float32 [2, 2, 1024, 16384], P(None, None, 'gy', 'gx')
The draws below stay inside these ranges and needn't reach their ends.
Inputs may be any that keep to these rules, and one draw needn't show every extreme that they name: `counts`: every tile has 1 to 12 live slots and some tile has exactly 12; tiles (2 * c, b) and (2 * c + 1, b) have at most 16 live slots together, and some such pair has exactly that many.
All inputs are finite; a program needn't handle non-finite values.
Results may differ from the reference program's by a relative error of at most 0.0003.
Values sent between devices are 32-bit elements; how exact they have to be, the bound alone decides.
No kernel may reach another device: no remote copies, remote signals or barrier semaphores. Data moves between devices by JAX's collectives and lax.ppermute only.
A program may use at most 64 MiB of HBM per device.

```python
import math
import jax
import jax.numpy as jnp
from jax import lax

W = 128
SL = 2
TR = 128
TC = 256
CAP = 12
PB = 8
NR = 1024
NC = 16384
N_GX = 64
N_GY = 8


def draw_counts(key, part):
    key = jax.random.fold_in(key, 11)
    subkeys = jax.random.split(key, 4)
    pair_count = N_GY // 2
    totals = jax.random.randint(subkeys[0], (pair_count, N_GX), 2, 2 * PB + 1)
    lowest = jnp.maximum(1, totals - CAP)
    highest = jnp.minimum(CAP, totals - 1)
    leading = jax.random.randint(subkeys[1], (pair_count, N_GX), lowest, highest + 1)
    chosen = jax.random.randint(subkeys[2], (), 0, pair_count * N_GX)
    heavy_side = jax.random.randint(subkeys[3], (), 0, 2)
    flat_index = jnp.arange(pair_count * N_GX, dtype=jnp.int32).reshape(pair_count, N_GX)
    forced = flat_index == chosen
    heavy_value = jnp.where(heavy_side == 0, CAP, 2 * PB - CAP)
    leading = jnp.where(forced, heavy_value, leading)
    totals = jnp.where(forced, 2 * PB, totals)
    trailing = totals - leading
    return jnp.stack([leading, trailing], axis=1).reshape(N_GY, N_GX).astype(jnp.int32)


def with_ends(entries, stream_key, smallest, largest):
    longest = entries.shape.index(max(entries.shape))
    spots = []
    for shift in (0, 1):
        where = [jax.random.randint(jax.random.fold_in(stream_key, axis), (), 0, length) for axis, length in enumerate(entries.shape)]
        where[longest] = (where[longest] + shift) % entries.shape[longest]
        spots.append(tuple(where))
    return entries.at[spots[0]].set(smallest).at[spots[1]].set(largest)


def levels(stream_key, shape, pieces, smallest, largest):
    def one(axis_at, shards_of):
        steps = jax.random.uniform(jax.random.fold_in(jax.random.fold_in(stream_key, 6), axis_at), (shards_of,), jnp.float32, smallest / len(pieces), largest / len(pieces))
        return jnp.repeat(jnp.exp(steps), shape[axis_at] // shards_of).reshape((-1,) + (1,) * (len(shape) - axis_at - 1))

    level = one(*pieces[0])
    for cut in pieces[1:]:
        level = level * one(*cut)
    return level


def normal_values(rng, extent, spread, limit, cuts=(), held_as=jnp.bfloat16):
    drawn = spread * jax.random.normal(rng, extent, jnp.float32)
    if cuts:
        drawn = drawn * levels(rng, extent, cuts, -0.22, 0.18)
    return jnp.clip(drawn, -limit, limit).astype(held_as)


def setup_inputs(seed: int = 0) -> dict:
    seeds = jax.random.split(jax.random.key(seed), 9)
    return {
        "object_field": normal_values(seeds[0], (2, SL, NR, NC), 0.8, 5.0, ((2, 8), (3, 64)), jnp.float32),
        "first_moment": normal_values(seeds[1], (2, SL, NR, NC), 0.3, 2.0, ((2, 8), (3, 64)), jnp.float32),
        "second_moment": jnp.clip(jnp.exp(math.log(4.0) - 2.9957323 * jax.random.uniform(seeds[2], (2, SL, NR, NC), jnp.float32) ** levels(seeds[2], (2, SL, NR, NC), ((2, 8), (3, 64)), -0.2, 0.2)), 0.2, 4.0),
        "probe_wave": normal_values(seeds[3], (2, W, W), 1.0, 5.0, (), jnp.float32),
        "patterns": jnp.clip(jnp.exp(math.log(5.0) - 4.6051702 * jax.random.uniform(seeds[4], (N_GY, N_GX * CAP, W, W), jnp.float32) ** levels(seeds[4], (N_GY, N_GX * CAP, W, W), ((0, 8), (1, 64)), -0.2, 0.2)), 0.05, 5.0),
        "row_offsets": with_ends(jax.random.randint(seeds[5], (N_GY, N_GX * CAP), 0, TR), jax.random.fold_in(seeds[5], 1), 0, TR - 1).astype(jnp.int32),
        "col_offsets": with_ends(jax.random.randint(seeds[6], (N_GY, N_GX * CAP), 0, TC), jax.random.fold_in(seeds[6], 1), 0, TC - 1).astype(jnp.int32),
        "counts": draw_counts(jax.random.fold_in(seeds[8], 71), 0),
    }


smoothing = 0.15
beta_first = 0.9
beta_second = 0.999
first_fix = 1.0 - 0.9 ** 2
second_fix = 1.0 - 0.999 ** 2
rate_scale = 0.25 * 1.2732395
misfit_weight = 1.0 / 64.0

def spectral_kernel(points):
    indices = jnp.arange(points, dtype=jnp.int32)
    frequency = jnp.where(indices < points // 2, indices, indices - points)
    squares = (frequency[:, None] * frequency[:, None] + frequency[None, :] * frequency[None, :]) % (8 * points)
    phases = -math.pi / (4.0 * points) * squares.astype(jnp.float32)
    return (jnp.cos(phases), jnp.sin(phases))

def slot_misfit(window, probe_wave, pattern, weight, kernel_real, kernel_imag):
    kernel = kernel_real + 1j * kernel_imag
    field_wave = probe_wave[0] + 1j * probe_wave[1]
    for depth_index in range(SL):
        field_wave = field_wave * (window[0, depth_index] + 1j * window[1, depth_index])
        if depth_index + 1 < SL:
            field_wave = jnp.fft.ifft2(jnp.fft.fft2(field_wave, norm='ortho') * kernel, norm='ortho')
    far_field = jnp.fft.fft2(field_wave, norm='ortho')
    misfit = jnp.real(far_field) ** 2 + jnp.imag(far_field) ** 2 - pattern
    return misfit_weight * weight * jnp.sum(misfit * misfit)

def reference(object_field, first_moment, second_moment, probe_wave, patterns, row_offsets, col_offsets, counts):
    total_rows = object_field.shape[2]
    total_cols = object_field.shape[3]
    padded = jnp.pad(object_field, ((0, 0), (0, 0), (0, W), (0, W)))
    kernel_real, kernel_imag = spectral_kernel(W)
    slot_gradient = jax.vmap(jax.grad(slot_misfit), in_axes=(0, None, 0, 0, None, None))
    anchor = jnp.zeros((), jnp.int32)

    def tile_step(running, flat_index):
        tile_row = flat_index // N_GX
        tile_col = flat_index % N_GX
        row_starts = lax.dynamic_slice(row_offsets, (tile_row, tile_col * CAP), (1, CAP))[0] + tile_row * TR
        col_starts = lax.dynamic_slice(col_offsets, (tile_row, tile_col * CAP), (1, CAP))[0] + tile_col * TC
        tile_patterns = lax.dynamic_slice(patterns, (tile_row, tile_col * CAP, anchor, anchor), (1, CAP, W, W))[0]
        live_count = lax.dynamic_slice(counts, (tile_row, tile_col), (1, 1))[0, 0]
        weights = (jnp.arange(CAP, dtype=jnp.int32) < live_count).astype(jnp.float32)

        def single_window(row_start, col_start):
            return lax.dynamic_slice(padded, (anchor, anchor, row_start, col_start), (2, SL, W, W))
        windows = jax.vmap(single_window)(row_starts, col_starts)
        slot_grads = slot_gradient(windows, probe_wave, tile_patterns, weights, kernel_real, kernel_imag)

        def add_slot(slot_index, running_sum):
            corner = (anchor, anchor, row_starts[slot_index], col_starts[slot_index])
            current = lax.dynamic_slice(running_sum, corner, (2, SL, W, W))
            return lax.dynamic_update_slice(running_sum, current + slot_grads[slot_index], corner)
        return (lax.fori_loop(0, CAP, add_slot, running), None)
    gradient_sum, unused = lax.scan(tile_step, jnp.zeros(padded.shape, jnp.float32), jnp.arange(N_GY * N_GX, dtype=jnp.int32))
    gradient = gradient_sum[:, :, :total_rows, :total_cols]
    rimmed = jnp.pad(gradient, ((0, 0), (0, 0), (1, 1), (1, 1)))
    laplace = rimmed[:, :, :-2, 1:-1] + rimmed[:, :, 2:, 1:-1] + rimmed[:, :, 1:-1, :-2] + rimmed[:, :, 1:-1, 2:] - 4.0 * gradient
    smoothed = gradient + smoothing * laplace
    new_first = beta_first * first_moment + (1.0 - beta_first) * smoothed
    new_second = beta_second * second_moment + (1.0 - beta_second) * smoothed * smoothed
    update_step = rate_scale * jnp.arctan2(new_first / first_fix, jnp.sqrt(new_second / second_fix))
    return (object_field - update_step, new_first, new_second)
```

```python
import functools
import math

import jax
import jax.numpy as jnp
import ml_dtypes
import numpy as np
from jax import lax
from jax.experimental import pallas as pl
from jax.experimental.pallas import tpu as pltpu
from jax.sharding import PartitionSpec as P

smoothing = 0.15
beta_first = 0.9
beta_second = 0.999
first_fix = 1.0 - 0.9**2
second_fix = 1.0 - 0.999**2
rate_scale = 0.25 * 1.2732395
misfit_weight = 1.0 / 64.0

W = 128
BATCH = 4
f32 = jnp.float32
bf16 = jnp.bfloat16
VMEM = pl.BlockSpec(memory_space=pltpu.VMEM)
SMEM = pl.BlockSpec(memory_space=pltpu.SMEM)


def embedded(matrix):
    return np.block([[matrix.real, matrix.imag], [-matrix.imag, matrix.real]])


def wave_tables():
    index = np.arange(W)
    angle = 2.0 * math.pi / W * (index[:, None] * index[None, :] % W)
    dft = (np.cos(angle) - 1j * np.sin(angle)) / math.sqrt(W)
    frequency = np.where(index < W // 2, index, index - W)
    hop = np.conj(dft) @ (np.exp(-1j * math.pi / 512.0 * frequency**2)[:, None] * dft)
    whole = np.stack([embedded(m) for m in (dft, np.conj(dft), hop, np.conj(hop))])
    high = whole.astype(ml_dtypes.bfloat16)
    low = (whole - high.astype(np.float64)).astype(ml_dtypes.bfloat16)
    return np.stack([high, low], axis=1)


DFT, DFT_CONJ, HOP, HOP_CONJ = range(4)
CONJ = (DFT_CONJ, DFT, HOP_CONJ, HOP)


def halves(values):
    high = values.astype(bf16)
    return high, (values - high.astype(f32)).astype(bf16)


def dot(a, b):
    return jnp.dot(a, b, preferred_element_type=f32)


def both_sides(waves, table, which):
    left = CONJ[which]
    columns = jnp.concatenate(
        [
            jnp.concatenate([re for re, im in waves], axis=1),
            jnp.concatenate([im for re, im in waves], axis=1),
        ],
        axis=0,
    )
    high, low = halves(columns)
    columns = dot(table[left, 0], high) + dot(table[left, 1], high) + dot(table[left, 0], low)
    rows = jnp.concatenate(
        [
            jnp.concatenate(
                [columns[:W, k * W : (k + 1) * W], columns[W:, k * W : (k + 1) * W]], axis=1
            )
            for k in range(len(waves))
        ],
        axis=0,
    )
    high, low = halves(rows)
    rows = dot(high, table[which, 0]) + dot(high, table[which, 1]) + dot(low, table[which, 0])
    return [
        (rows[k * W : (k + 1) * W, :W], rows[k * W : (k + 1) * W, W:]) for k in range(len(waves))
    ]


def times(a, b):
    return a[0] * b[0] - a[1] * b[1], a[0] * b[1] + a[1] * b[0]


def times_conj(a, b):
    return a[0] * b[0] + a[1] * b[1], a[1] * b[0] - a[0] * b[1]


def gradient_kernel(
    rows_ref,
    cols_ref,
    count_ref,
    edge_ref,
    here_ref,
    below_ref,
    right_ref,
    corner_ref,
    probe_ref,
    patterns_ref,
    table_ref,
    own_ref,
    down_ref,
    up_ref,
    side_ref,
    left_ref,
    obj,
    acc,
):
    for p in range(4):
        for t in range(2):
            obj[t, p, :W, :] = here_ref[p, :, t * W : (t + 1) * W]
            obj[t, p, W:, :] = below_ref[p, :, t * W : (t + 1) * W]
        obj[2, p, :W, :] = right_ref[p]
        obj[2, p, W:, :] = corner_ref[p]
    acc[...] = jnp.zeros_like(acc)
    lane = lax.broadcasted_iota(jnp.int32, (W, W), 1)
    count = count_ref[0, 0]

    def batch(step, carry):
        slots = [step * BATCH + j for j in range(BATCH)]
        places = []
        for k in slots:
            col = cols_ref[0, k]
            places.append((rows_ref[0, k], col // W, col % W))
        windows = []
        for row, tile, shift in places:
            planes = []
            for p in range(4):
                first = obj[tile, p, pl.ds(row, W), :]
                second = obj[tile + 1, p, pl.ds(row, W), :]
                chosen = jnp.where(lane >= shift, first, second)
                planes.append(pltpu.roll(chosen, (W - shift) % W, 1))
            windows.append(((planes[0], planes[2]), (planes[1], planes[3])))
        probe = (probe_ref[0], probe_ref[1])
        waves = [times(probe, window[0]) for window in windows]
        waves = both_sides(waves, table_ref, HOP)
        fars = both_sides([times(w, o[1]) for w, o in zip(waves, windows)], table_ref, DFT)
        back = []
        for k, far in zip(slots, fars):
            misfit = far[0] * far[0] + far[1] * far[1] - patterns_ref[k]
            misfit = misfit * jnp.where(k < count, 4.0 * misfit_weight, 0.0)
            back.append((misfit * far[0], misfit * far[1]))
        back = both_sides(back, table_ref, DFT_CONJ)
        second = [times_conj(g, w) for g, w in zip(back, waves)]
        back = both_sides([times_conj(g, o[1]) for g, o in zip(back, windows)], table_ref, HOP_CONJ)
        first = [times_conj(g, probe) for g in back]
        for (row, tile, shift), one, two in zip(places, first, second):
            for p, plane in enumerate((one[0], two[0], one[1], two[1])):
                turned = pltpu.roll(plane, shift, 1)
                at = pl.ds(row + 8, W)
                acc[tile, p, at, :] += jnp.where(lane >= shift, turned, 0.0)
                acc[tile + 1, p, at, :] += jnp.where(lane < shift, turned, 0.0)
        return carry

    lax.fori_loop(0, (count + BATCH - 1) // BATCH, batch, 0)

    @pl.when(edge_ref[0, 0] == 1)
    def _():
        acc[2] = jnp.zeros(acc.shape[1:], f32)

    @pl.when(edge_ref[0, 1] == 1)
    def _():
        acc[:, :, 8 + W :, :] = jnp.zeros((3, 4, acc.shape[2] - 8 - W, W), f32)

    lane = lax.broadcasted_iota(jnp.int32, (W, W), 1)
    down_ref[:, W:, :] = jnp.zeros((4, 8, 3 * W), f32)
    up_ref[...] = jnp.zeros_like(up_ref)
    left_ref[...] = jnp.zeros_like(left_ref)
    for p in range(4):
        for half in range(2):
            base = 8 + half * W
            centres = [acc[t, p, base : base + W, :] for t in range(3)]
            for t in range(3):
                above = acc[t, p, base - 1 : base - 1 + W, :]
                under = acc[t, p, base + 1 : base + 1 + W, :]
                before = pltpu.roll(centres[t], 1, 1)
                edge = pltpu.roll(centres[t - 1], 1, 1) if t else 0.0
                before = jnp.where(lane == 0, edge, before)
                after = pltpu.roll(centres[t], W - 1, 1)
                edge = pltpu.roll(centres[t + 1], W - 1, 1) if t < 2 else 0.0
                after = jnp.where(lane == W - 1, edge, after)
                smooth = centres[t] + smoothing * (
                    above + under + before + after - 4.0 * centres[t]
                )
                if half:
                    down_ref[p, :W, t * W : (t + 1) * W] = smooth
                elif t < 2:
                    own_ref[p, :, t * W : (t + 1) * W] = smooth
                else:
                    side_ref[p] = smooth
            rim = smoothing * centres[0].T[0:1, :]
            if half:
                down_ref[p, W : W + 1, :W] = rim
            else:
                left_ref[p : p + 1, :] = rim
        for t in range(3):
            up_ref[p : p + 1, t * W : (t + 1) * W] = smoothing * acc[t, p, 8:9, :]


def middle_kernel(side_ref, left_ref, above_ref, under_ref, side_out, left_out):
    for p in range(4):
        side_out[p] = side_ref[p] + above_ref[p, :W, 2 * W :]
        side_out[p, W - 1 : W, :] += under_ref[p : p + 1, 2 * W :]
    left_out[...] = left_ref[...]
    for p in range(4):
        left_out[p : p + 1, :] += above_ref[p, W : W + 1, :W]


def arc(slope):
    size = jnp.abs(slope)
    big = size > 2.414213562373095
    mid = size > 0.4142135623730950
    top = jnp.where(big, -1.0, jnp.where(mid, size - 1.0, size))
    low = jnp.where(big, size, jnp.where(mid, size + 1.0, 1.0))
    base = jnp.where(big, math.pi / 2, jnp.where(mid, math.pi / 4, 0.0))
    x = top / low
    z = x * x
    poly = (
        ((8.05374449538e-2 * z - 1.38776856032e-1) * z + 1.99777106478e-1) * z - 3.33329491539e-1
    ) * z * x + x
    value = base + poly
    return jnp.where(slope < 0.0, -value, value)


def update_kernel(
    obj_ref,
    first_ref,
    second_ref,
    own_ref,
    above_ref,
    under_ref,
    side_ref,
    left_ref,
    new_obj,
    new_first,
    new_second,
):
    row = lax.broadcasted_iota(jnp.int32, (W, W), 0)
    lane = lax.broadcasted_iota(jnp.int32, (W, W), 1)
    for p in range(4):
        for t in range(2):
            at = (p, slice(None), slice(t * W, (t + 1) * W))
            total = own_ref[at] + above_ref[p, :W, t * W : (t + 1) * W]
            total += jnp.where(row == W - 1, under_ref[p : p + 1, t * W : (t + 1) * W], 0.0)
            if t == 0:
                total += side_ref[p]
            else:
                column = jnp.broadcast_to(left_ref[p : p + 1, :], (W, W)).T
                total += jnp.where(lane == W - 1, column, 0.0)
            first = beta_first * first_ref[at] + (1.0 - beta_first) * total
            second = beta_second * second_ref[at] + (1.0 - beta_second) * total * total
            new_first[at] = first
            new_second[at] = second
            slope = (first * (1.0 / first_fix)) * lax.rsqrt(second * (1.0 / second_fix))
            new_obj[at] = obj_ref[at] - rate_scale * arc(slope)


def shift(block, axis, distance):
    count = lax.axis_size(axis)
    pairs = [(i + distance, i) for i in range(count) if 0 <= i + distance < count]
    return lax.ppermute(block, axis, pairs)


def call(kernel, outs, specs, scratch=()):
    return pl.pallas_call(
        kernel,
        out_shape=[jax.ShapeDtypeStruct(s, f32) for s in outs],
        in_specs=specs,
        out_specs=[VMEM] * len(outs),
        scratch_shapes=scratch,
        compiler_params=pltpu.CompilerParams(vmem_limit_bytes=40 * 1024 * 1024),
    )


def shards(
    object_field,
    first_moment,
    second_moment,
    probe_wave,
    patterns,
    row_offsets,
    col_offsets,
    counts,
    table,
):
    here = object_field.reshape(4, W, 2 * W)
    right = shift(here[:, :, :W], "gx", 1)
    below = shift(here, "gy", 1)
    corner = shift(right, "gy", 1)
    edge = jnp.stack(
        [
            lax.axis_index("gx") == lax.axis_size("gx") - 1,
            lax.axis_index("gy") == lax.axis_size("gy") - 1,
        ]
    ).astype(jnp.int32)[None]
    own, down, up, side, left = call(
        gradient_kernel,
        [(4, W, 2 * W), (4, W + 8, 3 * W), (8, 3 * W), (4, W, W), (8, W)],
        [SMEM] * 4 + [VMEM] * 7,
        [pltpu.VMEM((3, 4, 2 * W, W), f32), pltpu.VMEM((3, 4, 2 * W + 16, W), f32)],
    )(
        row_offsets,
        col_offsets,
        counts,
        edge,
        here,
        below,
        right,
        corner,
        probe_wave,
        patterns[0],
        table,
    )
    above = shift(down, "gy", -1)
    under = shift(up, "gy", 1)
    side, left = call(middle_kernel, [(4, W, W), (8, W)], [VMEM] * 4)(side, left, above, under)
    side = shift(side, "gx", -1)
    left = shift(left, "gx", 1)
    outs = call(update_kernel, [(4, W, 2 * W)] * 3, [VMEM] * 8)(
        here,
        first_moment.reshape(here.shape),
        second_moment.reshape(here.shape),
        own,
        above,
        under,
        side,
        left,
    )
    return tuple(out.reshape(object_field.shape) for out in outs)


def solution(mesh):
    whole = P(None, None, "gy", "gx")
    tiles = P("gy", "gx")
    body = jax.shard_map(
        shards,
        mesh=mesh,
        in_specs=(whole, whole, whole, P(), P("gy", "gx", None, None), tiles, tiles, tiles, P()),
        out_specs=(whole, whole, whole),
        check_vma=False,
    )

    def step(*args):
        return body(*args, jnp.asarray(wave_tables()))

    return step
```

```python
import math

import jax
import jax.numpy as jnp
import ml_dtypes
import numpy as np
from jax import lax
from jax.experimental import pallas as pl
from jax.experimental.pallas import tpu as pltpu
from jax.sharding import PartitionSpec as P

smoothing = 0.15
beta_first = 0.9
beta_second = 0.999
first_fix = 1.0 - 0.9**2
second_fix = 1.0 - 0.999**2
rate_scale = 0.25 * 1.2732395
misfit_weight = 1.0 / 64.0

W = 128
f32 = jnp.float32
bf16 = jnp.bfloat16
VMEM = pl.BlockSpec(memory_space=pltpu.VMEM)
SMEM = pl.BlockSpec(memory_space=pltpu.SMEM)
HBM = pl.BlockSpec(memory_space=pltpu.HBM)


def embedded(matrix):
    return np.block([[matrix.real, matrix.imag], [-matrix.imag, matrix.real]])


def wave_tables():
    index = np.arange(W)
    angle = 2.0 * math.pi / W * (index[:, None] * index[None, :] % W)
    dft = (np.cos(angle) - 1j * np.sin(angle)) / math.sqrt(W)
    frequency = np.where(index < W // 2, index, index - W)
    hop = np.conj(dft) @ (np.exp(-1j * math.pi / 512.0 * frequency**2)[:, None] * dft)
    whole = np.stack([embedded(m) for m in (dft, np.conj(dft), hop, np.conj(hop))])
    high = whole.astype(ml_dtypes.bfloat16)
    low = (whole - high.astype(np.float64)).astype(ml_dtypes.bfloat16)
    return np.stack([high, low], axis=1)


DFT, DFT_CONJ, HOP, HOP_CONJ = range(4)
CONJ = (DFT_CONJ, DFT, HOP_CONJ, HOP)


def halves(values):
    high = values.astype(bf16)
    return high, (values - high.astype(f32)).astype(bf16)


def dot(a, b):
    return jnp.dot(a, b, preferred_element_type=f32)


def both_sides(waves, table, which):
    left = CONJ[which]
    columns = jnp.concatenate(
        [
            jnp.concatenate([re for re, im in waves], axis=1),
            jnp.concatenate([im for re, im in waves], axis=1),
        ],
        axis=0,
    )
    high, low = halves(columns)
    columns = dot(table[left, 0], high) + dot(table[left, 1], high) + dot(table[left, 0], low)
    rows = jnp.concatenate(
        [
            jnp.concatenate(
                [columns[:W, k * W : (k + 1) * W], columns[W:, k * W : (k + 1) * W]], axis=1
            )
            for k in range(len(waves))
        ],
        axis=0,
    )
    high, low = halves(rows)
    rows = dot(high, table[which, 0]) + dot(high, table[which, 1]) + dot(low, table[which, 0])
    return [
        (rows[k * W : (k + 1) * W, :W], rows[k * W : (k + 1) * W, W:]) for k in range(len(waves))
    ]


def times(a, b):
    return a[0] * b[0] - a[1] * b[1], a[0] * b[1] + a[1] * b[0]


def times_conj(a, b):
    return a[0] * b[0] + a[1] * b[1], a[1] * b[0] - a[0] * b[1]


def fetch_kernel(patterns_ref, table_ref, probe_ref, patterns_out, table_out, probe_out, sems):
    pairs = [
        (patterns_ref, patterns_out),
        (table_ref, table_out),
        (probe_ref, probe_out),
    ]
    copies = [pltpu.make_async_copy(a, b, sems.at[i]) for i, (a, b) in enumerate(pairs)]
    for copy in copies:
        copy.start()
    for copy in copies:
        copy.wait()


def smoothed(acc, p, half, t):
    lane = lax.broadcasted_iota(jnp.int32, (W, W), 1)
    base = 8 + half * W
    centre = acc[t, p, base : base + W, :]
    above = acc[t, p, base - 1 : base - 1 + W, :]
    under = acc[t, p, base + 1 : base + 1 + W, :]
    before = pltpu.roll(centre, 1, 1)
    edge = pltpu.roll(acc[t - 1, p, base : base + W, :], 1, 1) if t else 0.0
    before = jnp.where(lane == 0, edge, before)
    after = pltpu.roll(centre, W - 1, 1)
    edge = pltpu.roll(acc[t + 1, p, base : base + W, :], W - 1, 1) if t < 2 else 0.0
    after = jnp.where(lane == W - 1, edge, after)
    return centre + smoothing * (above + under + before + after - 4.0 * centre)


def gradient_kernel(
    rows_ref,
    cols_ref,
    count_ref,
    edge_ref,
    here_ref,
    below_ref,
    right_ref,
    corner_ref,
    corner_too_ref,
    probe_ref,
    patterns_ref,
    table_ref,
    down_ref,
    up_ref,
    acc,
    obj,
):
    for p in range(4):
        for t in range(2):
            obj[t, p, :W, :] = here_ref[p, :, t * W : (t + 1) * W]
            obj[t, p, W:, :] = below_ref[p, :, t * W : (t + 1) * W]
        obj[2, p, :W, :] = right_ref[p]
        obj[2, p, W:, :] = corner_ref[p] + corner_too_ref[p]
    acc[...] = jnp.zeros_like(acc)
    lane = lax.broadcasted_iota(jnp.int32, (W, W), 1)
    count = count_ref[0, 0]

    def batch(slots):
        places = []
        for k in slots:
            col = cols_ref[0, k]
            places.append((rows_ref[0, k], col // W, col % W))
        windows = []
        for row, tile, shift in places:
            planes = []
            for p in range(4):
                first = obj[tile, p, pl.ds(row, W), :]
                second = obj[tile + 1, p, pl.ds(row, W), :]
                chosen = jnp.where(lane >= shift, first, second)
                planes.append(pltpu.roll(chosen, (W - shift) % W, 1))
            windows.append(((planes[0], planes[2]), (planes[1], planes[3])))
        probe = (probe_ref[0], probe_ref[1])
        waves = [times(probe, window[0]) for window in windows]
        waves = both_sides(waves, table_ref, HOP)
        fars = both_sides([times(w, o[1]) for w, o in zip(waves, windows)], table_ref, DFT)
        back = []
        for k, far in zip(slots, fars):
            misfit = far[0] * far[0] + far[1] * far[1] - patterns_ref[k]
            misfit = misfit * jnp.where(k < count, 4.0 * misfit_weight, 0.0)
            back.append((misfit * far[0], misfit * far[1]))
        back = both_sides(back, table_ref, DFT_CONJ)
        second = [times_conj(g, w) for g, w in zip(back, waves)]
        back = both_sides([times_conj(g, o[1]) for g, o in zip(back, windows)], table_ref, HOP_CONJ)
        first = [times_conj(g, probe) for g in back]
        for (row, tile, shift), one, two in zip(places, first, second):
            for p, plane in enumerate((one[0], two[0], one[1], two[1])):
                turned = pltpu.roll(plane, shift, 1)
                at = pl.ds(row + 8, W)
                acc[tile, p, at, :] += jnp.where(lane >= shift, turned, 0.0)
                acc[tile + 1, p, at, :] += jnp.where(lane < shift, turned, 0.0)

    @pl.when(count <= 6)
    def _():
        batch(range(6))

    @pl.when(count > 6)
    def _():
        batch(range(12))

    @pl.when(edge_ref[0, 0] == 1)
    def _():
        acc[2] = jnp.zeros(acc.shape[1:], f32)

    @pl.when(edge_ref[0, 1] == 1)
    def _():
        acc[:, :, 8 + W :, :] = jnp.zeros((3, 4, acc.shape[2] - 8 - W, W), f32)

    down_ref[:, W:, :] = jnp.zeros((4, 8, 3 * W), f32)
    up_ref[...] = jnp.zeros_like(up_ref)
    for p in range(4):
        for t in range(3):
            down_ref[p, :W, t * W : (t + 1) * W] = smoothed(acc, p, 1, t)
            up_ref[p : p + 1, t * W : (t + 1) * W] = smoothing * acc[t, p, 8:9, :]
        rim = smoothing * acc[0, p, 8 + W : 8 + 2 * W, :].T[0:1, :]
        down_ref[p, W : W + 1, :W] = rim


def rest_kernel(acc, own_ref, side_ref, left_ref):
    left_ref[...] = jnp.zeros_like(left_ref)
    for p in range(4):
        for t in range(2):
            own_ref[p, :, t * W : (t + 1) * W] = smoothed(acc, p, 0, t)
        side_ref[p] = smoothed(acc, p, 0, 2)
        left_ref[p : p + 1, :] = smoothing * acc[0, p, 8 : 8 + W, :].T[0:1, :]


def middle_kernel(side_ref, left_ref, above_ref, under_ref, side_out, left_out):
    for p in range(4):
        side_out[p] = side_ref[p] + above_ref[p, :W, 2 * W :]
        side_out[p, W - 1 : W, :] += under_ref[p : p + 1, 2 * W :]
    left_out[...] = left_ref[...]
    for p in range(4):
        left_out[p : p + 1, :] += above_ref[p, W : W + 1, :W]


def arc(slope):
    size = jnp.abs(slope)
    big = size > 2.414213562373095
    mid = size > 0.4142135623730950
    top = jnp.where(big, -1.0, jnp.where(mid, size - 1.0, size))
    low = jnp.where(big, size, jnp.where(mid, size + 1.0, 1.0))
    base = jnp.where(big, math.pi / 2, jnp.where(mid, math.pi / 4, 0.0))
    x = top / low
    z = x * x
    poly = (
        ((8.05374449538e-2 * z - 1.38776856032e-1) * z + 1.99777106478e-1) * z - 3.33329491539e-1
    ) * z * x + x
    value = base + poly
    return jnp.where(slope < 0.0, -value, value)


def update_kernel(
    obj_ref,
    first_ref,
    second_ref,
    own_ref,
    above_ref,
    under_ref,
    side_ref,
    left_ref,
    obj_out,
    first_out,
    second_out,
    results,
    sems,
):
    row = lax.broadcasted_iota(jnp.int32, (W, W), 0)
    lane = lax.broadcasted_iota(jnp.int32, (W, W), 1)
    copies = []
    for p in range(4):
        for t in range(2):
            at = (p, slice(None), slice(t * W, (t + 1) * W))
            total = own_ref[at] + above_ref[p, :W, t * W : (t + 1) * W]
            total += jnp.where(row == W - 1, under_ref[p : p + 1, t * W : (t + 1) * W], 0.0)
            if t == 0:
                total += side_ref[p]
            else:
                column = jnp.broadcast_to(left_ref[p : p + 1, :], (W, W)).T
                total += jnp.where(lane == W - 1, column, 0.0)
            first = beta_first * first_ref[at] + (1.0 - beta_first) * total
            second = beta_second * second_ref[at] + (1.0 - beta_second) * total * total
            slope = (first * (1.0 / first_fix)) * lax.rsqrt(second * (1.0 / second_fix))
            results[(0,) + at] = obj_ref[at] - rate_scale * arc(slope)
            results[(1,) + at] = first
            results[(2,) + at] = second
        for i, out in enumerate((obj_out, first_out, second_out)):
            copy = pltpu.make_async_copy(results.at[i, p], out.at[p], sems.at[i, p])
            copy.start()
            copies.append(copy)
    for copy in copies:
        copy.wait()


def permute(block, down, along, takes=None):
    rows, tiles = lax.axis_size("gy"), lax.axis_size("gx")
    pairs = []
    for b in range(tiles):
        for a in range(rows):
            there = 0 <= a + down < rows and 0 <= b + along < tiles
            if there and (takes is None or a % 2 == takes):
                pairs.append(((b + along) * rows + a + down, b * rows + a))
    return lax.ppermute(block, ("gx", "gy"), pairs)


def call(kernel, outs, ins, scratch=(), space=VMEM, flops=0, nbytes=0):
    return pl.pallas_call(
        kernel,
        out_shape=[jax.ShapeDtypeStruct(s, d) for s, d in outs],
        in_specs=ins,
        out_specs=[space] * len(outs),
        scratch_shapes=scratch,
        compiler_params=pltpu.CompilerParams(vmem_limit_bytes=40 * 1024 * 1024),
        cost_estimate=pl.CostEstimate(flops=flops, bytes_accessed=nbytes, transcendentals=0),
    )


def shards(
    object_field,
    first_moment,
    second_moment,
    probe_wave,
    patterns,
    row_offsets,
    col_offsets,
    counts,
    table,
):
    here = object_field.reshape(4, W, 2 * W)
    border = here[:, :, :W]
    right = permute(border, 0, 1)
    below = permute(here, 1, 0)
    corner = permute(border, 1, 1, 1)
    corner_too = permute(right, 1, 0, 0)
    edge = jnp.stack(
        [
            lax.axis_index("gx") == lax.axis_size("gx") - 1,
            lax.axis_index("gy") == lax.axis_size("gy") - 1,
        ]
    ).astype(jnp.int32)[None]
    fetched = call(
        fetch_kernel,
        [(patterns.shape[1:], f32), (table.shape, bf16), (probe_wave.shape, f32)],
        [HBM] * 3,
        [pltpu.SemaphoreType.DMA((3,))],
        nbytes=4 << 20,
    )(patterns[0], table, probe_wave)
    down, up, acc = call(
        gradient_kernel,
        [((4, W + 8, 3 * W), f32), ((8, 3 * W), f32), ((3, 4, 2 * W + 16, W), f32)],
        [SMEM] * 4 + [VMEM] * 8,
        [pltpu.VMEM((3, 4, 2 * W, W), f32)],
        flops=5 << 30,
        nbytes=8 << 20,
    )(
        row_offsets,
        col_offsets,
        counts,
        edge,
        here,
        below,
        right,
        corner,
        corner_too,
        fetched[2],
        fetched[0],
        fetched[1],
    )
    above = permute(down, -1, 0)
    under = permute(up, 1, 0)
    own, side, left = call(
        rest_kernel,
        [((4, W, 2 * W), f32), ((4, W, W), f32), ((8, W), f32)],
        [VMEM],
        flops=1 << 24,
        nbytes=2 << 20,
    )(acc)
    side, left = call(
        middle_kernel, [((4, W, W), f32), ((8, W), f32)], [VMEM] * 4, nbytes=1 << 20
    )(side, left, above, under)
    side = permute(side, 0, -1)
    left = permute(left, 0, 1)
    outs = call(
        update_kernel,
        [((4, W, 2 * W), f32)] * 3,
        [VMEM] * 8,
        [pltpu.VMEM((3, 4, W, 2 * W), f32), pltpu.SemaphoreType.DMA((3, 4))],
        HBM,
        flops=1 << 24,
        nbytes=4 << 20,
    )(
        here,
        first_moment.reshape(here.shape),
        second_moment.reshape(here.shape),
        own,
        above,
        under,
        side,
        left,
    )
    return tuple(out.reshape(object_field.shape) for out in outs)


def solution(mesh):
    whole = P(None, None, "gy", "gx")
    tiles = P("gy", "gx")
    body = jax.shard_map(
        shards,
        mesh=mesh,
        in_specs=(whole, whole, whole, P(), P("gy", "gx", None, None), tiles, tiles, tiles, P()),
        out_specs=(whole, whole, whole),
        check_vma=False,
    )

    def step(*args):
        return body(*args, jnp.asarray(wave_tables()))

    return step
```

```python
import math

import jax
import jax.numpy as jnp
import ml_dtypes
import numpy as np
from jax import lax
from jax.experimental import pallas as pl
from jax.experimental.pallas import tpu as pltpu
from jax.sharding import PartitionSpec as P

smoothing = 0.15
beta_first = 0.9
beta_second = 0.999
first_fix = 1.0 - 0.9**2
second_fix = 1.0 - 0.999**2
rate_scale = 0.25 * 1.2732395
misfit_weight = 1.0 / 64.0

W = 128
SIX = (range(3), range(3, 6))
TWELVE = (range(6), range(6, 12))
f32 = jnp.float32
bf16 = jnp.bfloat16
VMEM = pl.BlockSpec(memory_space=pltpu.VMEM)
SMEM = pl.BlockSpec(memory_space=pltpu.SMEM)
HBM = pl.BlockSpec(memory_space=pltpu.HBM)


def embedded(matrix):
    return np.block([[matrix.real, matrix.imag], [-matrix.imag, matrix.real]])


def wave_tables():
    index = np.arange(W)
    angle = 2.0 * math.pi / W * (index[:, None] * index[None, :] % W)
    dft = (np.cos(angle) - 1j * np.sin(angle)) / math.sqrt(W)
    frequency = np.where(index < W // 2, index, index - W)
    hop = np.conj(dft) @ (np.exp(-1j * math.pi / 512.0 * frequency**2)[:, None] * dft)
    whole = np.stack([embedded(m) for m in (dft, np.conj(dft), hop, np.conj(hop))])
    high = whole.astype(ml_dtypes.bfloat16)
    low = (whole - high.astype(np.float64)).astype(ml_dtypes.bfloat16)
    return np.stack([high, low], axis=1)


DFT, DFT_CONJ, HOP, HOP_CONJ = range(4)
CONJ = (DFT_CONJ, DFT, HOP_CONJ, HOP)


def halves(values):
    high = values.astype(bf16)
    return high, (values - high.astype(f32)).astype(bf16)


def dot(a, b):
    return jnp.dot(a, b, preferred_element_type=f32)


def both_sides(waves, table, which):
    left = CONJ[which]
    columns = jnp.concatenate(
        [
            jnp.concatenate([re for re, im in waves], axis=1),
            jnp.concatenate([im for re, im in waves], axis=1),
        ],
        axis=0,
    )
    high, low = halves(columns)
    columns = dot(table[left, 0], high) + dot(table[left, 1], high) + dot(table[left, 0], low)
    rows = jnp.concatenate(
        [
            jnp.concatenate(
                [columns[:W, k * W : (k + 1) * W], columns[W:, k * W : (k + 1) * W]], axis=1
            )
            for k in range(len(waves))
        ],
        axis=0,
    )
    high, low = halves(rows)
    rows = dot(high, table[which, 0]) + dot(high, table[which, 1]) + dot(low, table[which, 0])
    return [
        (rows[k * W : (k + 1) * W, :W], rows[k * W : (k + 1) * W, W:]) for k in range(len(waves))
    ]


def times(a, b):
    return a[0] * b[0] - a[1] * b[1], a[0] * b[1] + a[1] * b[0]


def times_conj(a, b):
    return a[0] * b[0] + a[1] * b[1], a[1] * b[0] - a[0] * b[1]


def fetch_kernel(patterns_ref, table_ref, probe_ref, patterns_out, table_out, probe_out, sems):
    pairs = [
        (patterns_ref, patterns_out),
        (table_ref, table_out),
        (probe_ref, probe_out),
    ]
    copies = [pltpu.make_async_copy(a, b, sems.at[i]) for i, (a, b) in enumerate(pairs)]
    for copy in copies:
        copy.start()
    for copy in copies:
        copy.wait()


def smoothed(acc, p, half, t):
    lane = lax.broadcasted_iota(jnp.int32, (W, W), 1)
    base = 8 + half * W
    centre = acc[t, p, base : base + W, :]
    above = acc[t, p, base - 1 : base - 1 + W, :]
    under = acc[t, p, base + 1 : base + 1 + W, :]
    before = pltpu.roll(centre, 1, 1)
    edge = pltpu.roll(acc[t - 1, p, base : base + W, :], 1, 1) if t else 0.0
    before = jnp.where(lane == 0, edge, before)
    after = pltpu.roll(centre, W - 1, 1)
    edge = pltpu.roll(acc[t + 1, p, base : base + W, :], W - 1, 1) if t < 2 else 0.0
    after = jnp.where(lane == W - 1, edge, after)
    return centre + smoothing * (above + under + before + after - 4.0 * centre)


def gradient_kernel(
    rows_ref,
    cols_ref,
    count_ref,
    edge_ref,
    here_ref,
    below_ref,
    right_ref,
    corner_ref,
    corner_too_ref,
    probe_ref,
    patterns_ref,
    table_ref,
    down_ref,
    across_ref,
    up_ref,
    acc,
    obj,
):
    for p in range(4):
        for t in range(2):
            obj[t, p, :W, :] = here_ref[p, :, t * W : (t + 1) * W]
            obj[t, p, W:, :] = below_ref[p, :, t * W : (t + 1) * W]
        obj[2, p, :W, :] = right_ref[p]
        obj[2, p, W:, :] = corner_ref[p] + corner_too_ref[p]
    acc[...] = jnp.zeros_like(acc)
    lane = lax.broadcasted_iota(jnp.int32, (W, W), 1)
    count = count_ref[0, 0]

    probe = (probe_ref[0], probe_ref[1])

    def place(k):
        col = cols_ref[0, k]
        return rows_ref[0, k], col // W, col % W

    def window(k, s):
        row, tile, shift = place(k)
        planes = []
        for p in (s, 2 + s):
            first = obj[tile, p, pl.ds(row, W), :]
            second = obj[tile + 1, p, pl.ds(row, W), :]
            chosen = jnp.where(lane >= shift, first, second)
            planes.append(pltpu.roll(chosen, (W - shift) % W, 1))
        return tuple(planes)

    def scatter(k, s, plane_pair):
        row, tile, shift = place(k)
        at = pl.ds(row + 8, W)
        for p, plane in zip((s, 2 + s), plane_pair):
            turned = pltpu.roll(plane, shift, 1)
            acc[tile, p, at, :] += jnp.where(lane >= shift, turned, 0.0)
            acc[tile + 1, p, at, :] += jnp.where(lane < shift, turned, 0.0)

    def hop(state):
        waves = [times(probe, window(k, 0)) for k in state["slots"]]
        state["waves"] = both_sides(waves, table_ref, HOP)

    def far(state):
        state["object"] = [window(k, 1) for k in state["slots"]]
        waves = [times(w, o) for w, o in zip(state["waves"], state["object"])]
        state["far"] = both_sides(waves, table_ref, DFT)

    def back(state):
        grads = []
        for k, wave in zip(state["slots"], state["far"]):
            misfit = wave[0] * wave[0] + wave[1] * wave[1] - patterns_ref[k]
            misfit = misfit * jnp.where(k < count, 4.0 * misfit_weight, 0.0)
            grads.append((misfit * wave[0], misfit * wave[1]))
        state["back"] = both_sides(grads, table_ref, DFT_CONJ)

    def hop_back(state):
        for k, g, w in zip(state["slots"], state["back"], state["waves"]):
            scatter(k, 1, times_conj(g, w))
        grads = [times_conj(g, o) for g, o in zip(state["back"], state["object"])]
        state["first"] = both_sides(grads, table_ref, HOP_CONJ)

    def finish(state):
        for k, g in zip(state["slots"], state["first"]):
            scatter(k, 0, times_conj(g, probe))

    def batch(groups):
        stages = (hop, far, back, hop_back, finish)
        states = [{"slots": slots} for slots in groups]
        for turn in range(len(stages) + len(states) - 1):
            for i, state in enumerate(states):
                if 0 <= turn - i < len(stages):
                    stages[turn - i](state)

    @pl.when(count <= 6)
    def _():
        batch(SIX)

    @pl.when(count > 6)
    def _():
        batch(TWELVE)

    @pl.when(edge_ref[0, 0] == 1)
    def _():
        acc[2] = jnp.zeros(acc.shape[1:], f32)

    @pl.when(edge_ref[0, 1] == 1)
    def _():
        acc[:, :, 8 + W :, :] = jnp.zeros((3, 4, acc.shape[2] - 8 - W, W), f32)

    across_ref[:, W:, :] = jnp.zeros((4, 8, W), f32)
    up_ref[...] = jnp.zeros_like(up_ref)
    for p in range(4):
        for t in range(2):
            down_ref[p, :, t * W : (t + 1) * W] = smoothed(acc, p, 1, t)
        across_ref[p, :W, :] = smoothed(acc, p, 1, 2)
        rim = smoothing * acc[0, p, 8 + W : 8 + 2 * W, :].T[0:1, :]
        across_ref[p, W : W + 1, :] = rim
        for t in range(3):
            up_ref[p : p + 1, t * W : (t + 1) * W] = smoothing * acc[t, p, 8:9, :]


def rest_kernel(acc, own_ref, side_ref, left_ref):
    left_ref[...] = jnp.zeros_like(left_ref)
    for p in range(4):
        for t in range(2):
            own_ref[p, :, t * W : (t + 1) * W] = smoothed(acc, p, 0, t)
        side_ref[p] = smoothed(acc, p, 0, 2)
        left_ref[p : p + 1, :] = smoothing * acc[0, p, 8 : 8 + W, :].T[0:1, :]


def middle_kernel(side_ref, left_ref, across_ref, under_ref, side_out, left_out):
    for p in range(4):
        side_out[p] = side_ref[p] + across_ref[p, :W, :]
        side_out[p, W - 1 : W, :] += under_ref[p : p + 1, 2 * W :]
    left_out[...] = left_ref[...]
    for p in range(4):
        left_out[p : p + 1, :] += across_ref[p, W : W + 1, :]


def arc(slope):
    size = jnp.abs(slope)
    big = size > 2.414213562373095
    mid = size > 0.4142135623730950
    top = jnp.where(big, -1.0, jnp.where(mid, size - 1.0, size))
    low = jnp.where(big, size, jnp.where(mid, size + 1.0, 1.0))
    base = jnp.where(big, math.pi / 2, jnp.where(mid, math.pi / 4, 0.0))
    x = top / low
    z = x * x
    poly = (
        ((8.05374449538e-2 * z - 1.38776856032e-1) * z + 1.99777106478e-1) * z - 3.33329491539e-1
    ) * z * x + x
    value = base + poly
    return jnp.where(slope < 0.0, -value, value)


def updated(t, refs, total, results, outs, sems, p):
    at = (p, slice(None), slice(t * W, (t + 1) * W))
    obj_ref, first_ref, second_ref = refs
    first = beta_first * first_ref[at] + (1.0 - beta_first) * total
    second = beta_second * second_ref[at] + (1.0 - beta_second) * total * total
    slope = (first * (1.0 / first_fix)) * lax.rsqrt(second * (1.0 / second_fix))
    results[0, p] = obj_ref[at] - rate_scale * arc(slope)
    results[1, p] = first
    results[2, p] = second
    copies = []
    for i, out in enumerate(outs):
        copy = pltpu.make_async_copy(results.at[i, p], out.at[at], sems.at[i, p])
        copy.start()
        copies.append(copy)
    return copies


def right_update_kernel(
    obj_ref, first_ref, second_ref, own_ref, above_ref, under_ref, left_ref, *outs_and_scratch
):
    *outs, results, sems = outs_and_scratch
    row = lax.broadcasted_iota(jnp.int32, (W, W), 0)
    lane = lax.broadcasted_iota(jnp.int32, (W, W), 1)
    copies = []
    for p in range(4):
        total = own_ref[p, :, W:] + above_ref[p, :, W:]
        total += jnp.where(row == W - 1, under_ref[p : p + 1, W : 2 * W], 0.0)
        column = jnp.broadcast_to(left_ref[p : p + 1, :], (W, W)).T
        total += jnp.where(lane == W - 1, column, 0.0)
        copies += updated(1, (obj_ref, first_ref, second_ref), total, results, outs, sems, p)
    for copy in copies:
        copy.wait()


def left_update_kernel(
    obj_ref, first_ref, second_ref, own_ref, above_ref, under_ref, side_ref, *outs_and_scratch
):
    *outs, results, sems = outs_and_scratch[3:]
    row = lax.broadcasted_iota(jnp.int32, (W, W), 0)
    copies = []
    for p in range(4):
        total = own_ref[p, :, :W] + above_ref[p, :, :W] + side_ref[p]
        total += jnp.where(row == W - 1, under_ref[p : p + 1, :W], 0.0)
        copies += updated(0, (obj_ref, first_ref, second_ref), total, results, outs, sems, p)
    for copy in copies:
        copy.wait()


def permute(block, down, along, takes=None):
    rows, tiles = lax.axis_size("gy"), lax.axis_size("gx")
    pairs = []
    for b in range(tiles):
        for a in range(rows):
            there = 0 <= a + down < rows and 0 <= b + along < tiles
            if there and (takes is None or a % 2 == takes):
                pairs.append(((b + along) * rows + a + down, b * rows + a))
    return lax.ppermute(block, ("gx", "gy"), pairs)


def call(kernel, outs, ins, scratch=(), space=VMEM, flops=0, nbytes=0, aliases=None):
    return pl.pallas_call(
        kernel,
        out_shape=[jax.ShapeDtypeStruct(s, d) for s, d in outs],
        in_specs=ins,
        out_specs=[space] * len(outs),
        scratch_shapes=scratch,
        input_output_aliases=aliases or {},
        compiler_params=pltpu.CompilerParams(vmem_limit_bytes=40 * 1024 * 1024),
        cost_estimate=pl.CostEstimate(flops=flops, bytes_accessed=nbytes, transcendentals=0),
    )


def shards(
    object_field,
    first_moment,
    second_moment,
    probe_wave,
    patterns,
    row_offsets,
    col_offsets,
    counts,
    table,
):
    here = object_field.reshape(4, W, 2 * W)
    border = here[:, :, :W]
    right = permute(border, 0, 1)
    below = permute(here, 1, 0)
    corner = permute(border, 1, 1, 1)
    corner_too = permute(right, 1, 0, 0)
    edge = jnp.stack(
        [
            lax.axis_index("gx") == lax.axis_size("gx") - 1,
            lax.axis_index("gy") == lax.axis_size("gy") - 1,
        ]
    ).astype(jnp.int32)[None]
    fetched = call(
        fetch_kernel,
        [(patterns.shape[1:], f32), (table.shape, bf16), (probe_wave.shape, f32)],
        [HBM] * 3,
        [pltpu.SemaphoreType.DMA((3,))],
        nbytes=4 << 20,
    )(*(pltpu.with_memory_space_constraint(x, pltpu.HBM) for x in (patterns[0], table, probe_wave)))
    down, across, up, acc = call(
        gradient_kernel,
        [
            ((4, W, 2 * W), f32),
            ((4, W + 8, W), f32),
            ((8, 3 * W), f32),
            ((3, 4, 2 * W + 16, W), f32),
        ],
        [SMEM] * 4 + [VMEM] * 8,
        [pltpu.VMEM((3, 4, 2 * W, W), f32)],
        flops=5 << 30,
        nbytes=8 << 20,
    )(
        row_offsets,
        col_offsets,
        counts,
        edge,
        here,
        below,
        right,
        corner,
        corner_too,
        fetched[2],
        fetched[0],
        fetched[1],
    )
    across = permute(across, -1, 0)
    above = permute(down, -1, 0)
    under = permute(up, 1, 0)
    own, side, left = call(
        rest_kernel,
        [((4, W, 2 * W), f32), ((4, W, W), f32), ((8, W), f32)],
        [VMEM],
        flops=1 << 24,
        nbytes=2 << 20,
    )(acc)
    side, left = call(
        middle_kernel, [((4, W, W), f32), ((8, W), f32)], [VMEM] * 4, nbytes=1 << 20
    )(side, left, across, under)
    left = permute(left, 0, 1)
    side = permute(side, 0, -1)
    moments = first_moment.reshape(here.shape), second_moment.reshape(here.shape)
    scratch = [pltpu.VMEM((3, 4, W, W), f32), pltpu.SemaphoreType.DMA((3, 4))]
    whole = [((4, W, 2 * W), f32)] * 3
    outs = call(
        right_update_kernel, whole, [VMEM] * 7, scratch, HBM, flops=1 << 24, nbytes=2 << 20
    )(here, *moments, own, above, under, left)
    outs = call(
        left_update_kernel,
        whole,
        [VMEM] * 7 + [HBM] * 3,
        scratch,
        HBM,
        flops=1 << 24,
        nbytes=2 << 20,
        aliases={7: 0, 8: 1, 9: 2},
    )(here, *moments, own, above, under, side, *outs)
    return tuple(out.reshape(object_field.shape) for out in outs)


def solution(mesh):
    whole = P(None, None, "gy", "gx")
    tiles = P("gy", "gx")
    body = jax.shard_map(
        shards,
        mesh=mesh,
        in_specs=(whole, whole, whole, P(), P("gy", "gx", None, None), tiles, tiles, tiles, P()),
        out_specs=(whole, whole, whole),
        check_vma=False,
    )

    def step(*args):
        return body(*args, jnp.asarray(wave_tables()))

    return step
```

```python
import math

import jax
import jax.numpy as jnp
import ml_dtypes
import numpy as np
from jax import lax
from jax.experimental import pallas as pl
from jax.experimental.pallas import tpu as pltpu
from jax.sharding import PartitionSpec as P

smoothing = 0.15
beta_first = 0.9
beta_second = 0.999
first_fix = 1.0 - 0.9**2
second_fix = 1.0 - 0.999**2
rate_scale = 0.25 * 1.2732395
misfit_weight = 1.0 / 64.0

W = 128
SIX = (range(3), range(3, 6))
TWELVE = (range(6), range(6, 12))
f32 = jnp.float32
bf16 = jnp.bfloat16
VMEM = pl.BlockSpec(memory_space=pltpu.VMEM)
SMEM = pl.BlockSpec(memory_space=pltpu.SMEM)
HBM = pl.BlockSpec(memory_space=pltpu.HBM)


def embedded(matrix):
    return np.block([[matrix.real, matrix.imag], [-matrix.imag, matrix.real]])


def wave_tables():
    index = np.arange(W)
    angle = 2.0 * math.pi / W * (index[:, None] * index[None, :] % W)
    dft = (np.cos(angle) - 1j * np.sin(angle)) / math.sqrt(W)
    frequency = np.where(index < W // 2, index, index - W)
    hop = np.conj(dft) @ (np.exp(-1j * math.pi / 512.0 * frequency**2)[:, None] * dft)
    whole = np.stack([embedded(m) for m in (dft, np.conj(dft), hop, np.conj(hop))])
    high = whole.astype(ml_dtypes.bfloat16)
    low = (whole - high.astype(np.float64)).astype(ml_dtypes.bfloat16)
    return np.stack([high, low], axis=1)


DFT, DFT_CONJ, HOP, HOP_CONJ = range(4)
CONJ = (DFT_CONJ, DFT, HOP_CONJ, HOP)


def halves(values):
    high = values.astype(bf16)
    return high, (values - high.astype(f32)).astype(bf16)


def dot(a, b):
    return jnp.dot(a, b, preferred_element_type=f32)


def both_sides(waves, table, which):
    left = CONJ[which]
    columns = jnp.concatenate(
        [
            jnp.concatenate([re for re, im in waves], axis=1),
            jnp.concatenate([im for re, im in waves], axis=1),
        ],
        axis=0,
    )
    high, low = halves(columns)
    columns = dot(table[left, 0], high) + dot(table[left, 1], high) + dot(table[left, 0], low)
    rows = jnp.concatenate(
        [
            jnp.concatenate(
                [columns[:W, k * W : (k + 1) * W], columns[W:, k * W : (k + 1) * W]], axis=1
            )
            for k in range(len(waves))
        ],
        axis=0,
    )
    high, low = halves(rows)
    rows = dot(high, table[which, 0]) + dot(high, table[which, 1]) + dot(low, table[which, 0])
    return [
        (rows[k * W : (k + 1) * W, :W], rows[k * W : (k + 1) * W, W:]) for k in range(len(waves))
    ]


def times(a, b):
    return a[0] * b[0] - a[1] * b[1], a[0] * b[1] + a[1] * b[0]


def times_conj(a, b):
    return a[0] * b[0] + a[1] * b[1], a[1] * b[0] - a[0] * b[1]


def fetch_kernel(patterns_ref, table_ref, probe_ref, patterns_out, table_out, probe_out, sems):
    pairs = [
        (patterns_ref, patterns_out),
        (table_ref, table_out),
        (probe_ref, probe_out),
    ]
    copies = [pltpu.make_async_copy(a, b, sems.at[i]) for i, (a, b) in enumerate(pairs)]
    for copy in copies:
        copy.start()
    for copy in copies:
        copy.wait()


def smoothed(acc, p, half, t):
    lane = lax.broadcasted_iota(jnp.int32, (W, W), 1)
    base = 8 + half * W
    centre = acc[t, p, base : base + W, :]
    above = acc[t, p, base - 1 : base - 1 + W, :]
    under = acc[t, p, base + 1 : base + 1 + W, :]
    before = pltpu.roll(centre, 1, 1)
    edge = pltpu.roll(acc[t - 1, p, base : base + W, :], 1, 1) if t else 0.0
    before = jnp.where(lane == 0, edge, before)
    after = pltpu.roll(centre, W - 1, 1)
    edge = pltpu.roll(acc[t + 1, p, base : base + W, :], W - 1, 1) if t < 2 else 0.0
    after = jnp.where(lane == W - 1, edge, after)
    return centre + smoothing * (above + under + before + after - 4.0 * centre)


def gradient_kernel(
    rows_ref,
    cols_ref,
    count_ref,
    edge_ref,
    here_ref,
    below_ref,
    right_ref,
    corner_ref,
    corner_too_ref,
    probe_ref,
    patterns_ref,
    table_ref,
    down_ref,
    across_ref,
    up_ref,
    acc,
    obj,
):
    for p in range(4):
        for t in range(2):
            obj[t, p, :W, :] = here_ref[p, :, t * W : (t + 1) * W]
            obj[t, p, W:, :] = below_ref[p, :, t * W : (t + 1) * W]
        obj[2, p, :W, :] = right_ref[p]
        obj[2, p, W:, :] = corner_ref[p] + corner_too_ref[p]
    acc[...] = jnp.zeros_like(acc)
    lane = lax.broadcasted_iota(jnp.int32, (W, W), 1)
    count = count_ref[0, 0]

    probe = (probe_ref[0], probe_ref[1])

    def place(k):
        col = cols_ref[0, k]
        return rows_ref[0, k], col // W, col % W

    def window(k, s):
        row, tile, shift = place(k)
        planes = []
        for p in (s, 2 + s):
            first = obj[tile, p, pl.ds(row, W), :]
            second = obj[tile + 1, p, pl.ds(row, W), :]
            chosen = jnp.where(lane >= shift, first, second)
            planes.append(pltpu.roll(chosen, (W - shift) % W, 1))
        return tuple(planes)

    def scatter(k, s, plane_pair):
        row, tile, shift = place(k)
        at = pl.ds(row + 8, W)
        for p, plane in zip((s, 2 + s), plane_pair):
            turned = pltpu.roll(plane, shift, 1)
            acc[tile, p, at, :] += jnp.where(lane >= shift, turned, 0.0)
            acc[tile + 1, p, at, :] += jnp.where(lane < shift, turned, 0.0)

    def hop(state):
        waves = [times(probe, window(k, 0)) for k in state["slots"]]
        state["waves"] = both_sides(waves, table_ref, HOP)

    def far(state):
        state["object"] = [window(k, 1) for k in state["slots"]]
        waves = [times(w, o) for w, o in zip(state["waves"], state["object"])]
        state["far"] = both_sides(waves, table_ref, DFT)

    def back(state):
        grads = []
        for k, wave in zip(state["slots"], state["far"]):
            misfit = wave[0] * wave[0] + wave[1] * wave[1] - patterns_ref[k]
            misfit = misfit * jnp.where(k < count, 4.0 * misfit_weight, 0.0)
            grads.append((misfit * wave[0], misfit * wave[1]))
        state["back"] = both_sides(grads, table_ref, DFT_CONJ)

    def hop_back(state):
        for k, g, w in zip(state["slots"], state["back"], state["waves"]):
            scatter(k, 1, times_conj(g, w))
        grads = [times_conj(g, o) for g, o in zip(state["back"], state["object"])]
        state["first"] = both_sides(grads, table_ref, HOP_CONJ)

    def finish(state):
        for k, g in zip(state["slots"], state["first"]):
            scatter(k, 0, times_conj(g, probe))

    def batch(groups):
        stages = (hop, far, back, hop_back, finish)
        states = [{"slots": slots} for slots in groups]
        for turn in range(len(stages) + len(states) - 1):
            for i, state in enumerate(states):
                if 0 <= turn - i < len(stages):
                    stages[turn - i](state)

    @pl.when(count <= 6)
    def _():
        batch(SIX)

    @pl.when(count > 6)
    def _():
        batch(TWELVE)

    @pl.when(edge_ref[0, 0] == 1)
    def _():
        acc[2] = jnp.zeros(acc.shape[1:], f32)

    @pl.when(edge_ref[0, 1] == 1)
    def _():
        acc[:, :, 8 + W :, :] = jnp.zeros((3, 4, acc.shape[2] - 8 - W, W), f32)

    across_ref[:, W:, :] = jnp.zeros((4, 8, W), f32)
    up_ref[...] = jnp.zeros_like(up_ref)
    for p in range(4):
        for t in range(2):
            down_ref[p, :, t * W : (t + 1) * W] = smoothed(acc, p, 1, t)
        across_ref[p, :W, :] = smoothed(acc, p, 1, 2)
        rim = smoothing * acc[0, p, 8 + W : 8 + 2 * W, :].T[0:1, :]
        across_ref[p, W : W + 1, :] = rim
        for t in range(3):
            up_ref[p : p + 1, t * W : (t + 1) * W] = smoothing * acc[t, p, 8:9, :]


def rest_kernel(acc, under_ref, own_ref, side_ref, left_ref):
    left_ref[...] = jnp.zeros_like(left_ref)
    for p in range(4):
        for t in range(2):
            own_ref[p, :, t * W : (t + 1) * W] = smoothed(acc, p, 0, t)
        own_ref[p, W - 1 : W, :] += under_ref[p : p + 1, : 2 * W]
        side_ref[p] = smoothed(acc, p, 0, 2)
        side_ref[p, W - 1 : W, :] += under_ref[p : p + 1, 2 * W :]
        left_ref[p : p + 1, :] = smoothing * acc[0, p, 8 : 8 + W, :].T[0:1, :]


def middle_kernel(side_ref, left_ref, across_ref, side_out, left_out):
    for p in range(4):
        side_out[p] = side_ref[p] + across_ref[p, :W, :]
    left_out[...] = left_ref[...]
    for p in range(4):
        left_out[p : p + 1, :] += across_ref[p, W : W + 1, :]


def arc(slope):
    size = jnp.abs(slope)
    big = size > 2.414213562373095
    mid = size > 0.4142135623730950
    top = jnp.where(big, -1.0, jnp.where(mid, size - 1.0, size))
    low = jnp.where(big, size, jnp.where(mid, size + 1.0, 1.0))
    base = jnp.where(big, math.pi / 2, jnp.where(mid, math.pi / 4, 0.0))
    x = top / low
    z = x * x
    poly = (
        ((8.05374449538e-2 * z - 1.38776856032e-1) * z + 1.99777106478e-1) * z - 3.33329491539e-1
    ) * z * x + x
    value = base + poly
    return jnp.where(slope < 0.0, -value, value)


def updated(t, refs, total, results, outs, sems, p):
    at = (p, slice(None), slice(t * W, (t + 1) * W))
    obj_ref, first_ref, second_ref = refs
    first = beta_first * first_ref[at] + (1.0 - beta_first) * total
    second = beta_second * second_ref[at] + (1.0 - beta_second) * total * total
    slope = (first * (1.0 / first_fix)) * lax.rsqrt(second * (1.0 / second_fix))
    results[0, p] = obj_ref[at] - rate_scale * arc(slope)
    results[1, p] = first
    results[2, p] = second
    copies = []
    for i, out in enumerate(outs):
        copy = pltpu.make_async_copy(results.at[i, p], out.at[at], sems.at[i, p])
        copy.start()
        copies.append(copy)
    return copies


def right_update_kernel(
    obj_ref, first_ref, second_ref, own_ref, above_ref, left_ref, *outs_and_scratch
):
    *outs, results, sems = outs_and_scratch
    lane = lax.broadcasted_iota(jnp.int32, (W, W), 1)
    copies = []
    for p in range(4):
        total = own_ref[p, :, W:] + above_ref[p, :, W:]
        column = jnp.broadcast_to(left_ref[p : p + 1, :], (W, W)).T
        total += jnp.where(lane == W - 1, column, 0.0)
        copies += updated(1, (obj_ref, first_ref, second_ref), total, results, outs, sems, p)
    for copy in copies:
        copy.wait()


def left_update_kernel(
    obj_ref, first_ref, second_ref, own_ref, above_ref, side_ref, *outs_and_scratch
):
    *outs, results, sems = outs_and_scratch[3:]
    copies = []
    for p in range(4):
        total = own_ref[p, :, :W] + above_ref[p, :, :W] + side_ref[p]
        copies += updated(0, (obj_ref, first_ref, second_ref), total, results, outs, sems, p)
    for copy in copies:
        copy.wait()


def permute(block, down, along, takes=None):
    rows, tiles = lax.axis_size("gy"), lax.axis_size("gx")
    pairs = []
    for b in range(tiles):
        for a in range(rows):
            there = 0 <= a + down < rows and 0 <= b + along < tiles
            if there and (takes is None or a % 2 == takes):
                pairs.append(((b + along) * rows + a + down, b * rows + a))
    return lax.ppermute(block, ("gx", "gy"), pairs)


def call(kernel, outs, ins, scratch=(), space=VMEM, flops=0, nbytes=0, aliases=None):
    return pl.pallas_call(
        kernel,
        out_shape=[jax.ShapeDtypeStruct(s, d) for s, d in outs],
        in_specs=ins,
        out_specs=[space] * len(outs),
        scratch_shapes=scratch,
        input_output_aliases=aliases or {},
        compiler_params=pltpu.CompilerParams(vmem_limit_bytes=40 * 1024 * 1024),
        cost_estimate=pl.CostEstimate(flops=flops, bytes_accessed=nbytes, transcendentals=0),
    )


def shards(
    object_field,
    first_moment,
    second_moment,
    probe_wave,
    patterns,
    row_offsets,
    col_offsets,
    counts,
    table,
):
    here = object_field.reshape(4, W, 2 * W)
    border = here[:, :, :W]
    right = permute(border, 0, 1)
    below = permute(here, 1, 0)
    corner = permute(border, 1, 1, 1)
    corner_too = permute(right, 1, 0, 0)
    edge = jnp.stack(
        [
            lax.axis_index("gx") == lax.axis_size("gx") - 1,
            lax.axis_index("gy") == lax.axis_size("gy") - 1,
        ]
    ).astype(jnp.int32)[None]
    fetched = call(
        fetch_kernel,
        [(patterns.shape[1:], f32), (table.shape, bf16), (probe_wave.shape, f32)],
        [HBM] * 3,
        [pltpu.SemaphoreType.DMA((3,))],
        nbytes=4 << 20,
    )(*(pltpu.with_memory_space_constraint(x, pltpu.HBM) for x in (patterns[0], table, probe_wave)))
    down, across, up, acc = call(
        gradient_kernel,
        [
            ((4, W, 2 * W), f32),
            ((4, W + 8, W), f32),
            ((8, 3 * W), f32),
            ((3, 4, 2 * W + 16, W), f32),
        ],
        [SMEM] * 4 + [VMEM] * 8,
        [pltpu.VMEM((3, 4, 2 * W, W), f32)],
        flops=5 << 30,
        nbytes=8 << 20,
    )(
        row_offsets,
        col_offsets,
        counts,
        edge,
        here,
        below,
        right,
        corner,
        corner_too,
        fetched[2],
        fetched[0],
        fetched[1],
    )
    across = permute(across, -1, 0)
    above = permute(down, -1, 0)
    under = permute(up, 1, 0)
    own, side, left = call(
        rest_kernel,
        [((4, W, 2 * W), f32), ((4, W, W), f32), ((8, W), f32)],
        [VMEM] * 2,
        flops=1 << 33,
        nbytes=2 << 20,
    )(acc, under)
    side, left = call(
        middle_kernel, [((4, W, W), f32), ((8, W), f32)], [VMEM] * 3, nbytes=1 << 20
    )(side, left, across)
    left = permute(left, 0, 1)
    side = permute(side, 0, -1)
    moments = first_moment.reshape(here.shape), second_moment.reshape(here.shape)
    scratch = [pltpu.VMEM((3, 4, W, W), f32), pltpu.SemaphoreType.DMA((3, 4))]
    whole = [((4, W, 2 * W), f32)] * 3
    outs = call(
        right_update_kernel, whole, [VMEM] * 6, scratch, HBM, flops=1 << 24, nbytes=2 << 20
    )(here, *moments, own, above, left)
    outs = call(
        left_update_kernel,
        whole,
        [VMEM] * 6 + [HBM] * 3,
        scratch,
        HBM,
        flops=1 << 24,
        nbytes=2 << 20,
        aliases={6: 0, 7: 1, 8: 2},
    )(here, *moments, own, above, side, *outs)
    return tuple(out.reshape(object_field.shape) for out in outs)


def solution(mesh):
    whole = P(None, None, "gy", "gx")
    tiles = P("gy", "gx")
    body = jax.shard_map(
        shards,
        mesh=mesh,
        in_specs=(whole, whole, whole, P(), P("gy", "gx", None, None), tiles, tiles, tiles, P()),
        out_specs=(whole, whole, whole),
        check_vma=False,
    )

    def step(*args):
        return body(*args, jnp.asarray(wave_tables()))

    return step
```
